512 devices in a mesh: replica: 64 (over x, z), fsdp: 8 (over y, core).
Axes of the slice: x: 4, y: 4, z: 16, core: 2. Of those that a mesh axis runs over, the one named last changes fastest.
Arguments:
- anchor: bfloat16 [64, 2, 256, 8192], P('replica', None, 'fsdp'), may hold values from -0.0625 to 0.0625
- local_params: bfloat16 [64, 2, 256, 8192], P('replica', None, 'fsdp'), as said below
- staleness: int32 [64], replicated, may hold values from 0 to 15
- master: float32 [2, 256, 8192], P(None, 'fsdp', 'replica'), may hold values from -0.0625 to 0.0625
- momentum: float32 [2, 256, 8192], P(None, 'fsdp', 'replica'), may hold values from -0.006 to 0.006
Outputs:
- new_global: bfloat16 [2, 256, 8192], P(None, 'fsdp')
- new_master: float32 [2, 256, 8192], P(None, 'fsdp', 'replica')
- new_momentum: float32 [2, 256, 8192], P(None, 'fsdp', 'replica')
The draws below stay inside these ranges and needn't reach their ends.
Inputs may be any that keep to these rules, and one draw needn't show every extreme that they name: `local_params`: a replica's parameters after its inner steps.
All inputs are finite; a program needn't handle non-finite values.
Results may differ from the reference program's by a relative error of at most 0.0022.
Values may be sent and summed in bfloat16 or wider, within the bound.
No kernel may reach another device: no remote copies, remote signals or barrier semaphores. Data moves between devices by JAX's collectives and lax.ppermute only.
A program may use at most 64 MiB of HBM per device.

```python
import jax
import jax.numpy as jnp
from jax import lax

D = 8192
ROWS = 256
REPLICAS = 64


def draw_local_params(key, part):
    key = jax.random.fold_in(key, 11)
    row_key, col_key, base_key = jax.random.split(key, 3)
    row_scale = jnp.exp(jax.random.uniform(row_key, (1, 1, ROWS, 1), jnp.float32, 0.0, 2.4))
    col_scale = jnp.exp(jax.random.uniform(col_key, (1, 1, 1, D), jnp.float32, 0.0, 2.4))
    values = jax.random.normal(base_key, (REPLICAS, 2, ROWS, D), jnp.float32)
    return (0.004 * row_scale * col_scale * values).astype(jnp.bfloat16)


def place_ends(array, stream_key, least, largest):
    longest = array.shape.index(max(array.shape))
    spots = []
    for shift in (0, 1):
        where = [jax.random.randint(jax.random.fold_in(stream_key, axis), (), 0, length) for axis, length in enumerate(array.shape)]
        where[longest] = (where[longest] + shift) % array.shape[longest]
        spots.append(tuple(where))
    return array.at[spots[0]].set(least).at[spots[1]].set(largest)


def shard_levels(key, dims, cuts, low, top_value):
    factor_of, own = 1.0, jax.random.fold_in(key, 6)
    for position, blocks in cuts:
        draws = jnp.exp(jax.random.uniform(jax.random.fold_in(own, position), (blocks,), jnp.float32, low / len(cuts), top_value / len(cuts)))
        factor_of = factor_of * jnp.repeat(draws, dims[position] // blocks).reshape([-1 if axis == position else 1 for axis in range(len(dims))])
    return factor_of


def noise(key, extent, width, most, shards=(), dtype=jnp.bfloat16):
    result = jax.random.normal(key, extent, jnp.float32) * width
    if len(shards) > 0:
        result = shard_levels(key, extent, shards, -0.22, 0.18) * result
    return jnp.clip(result, min=-most, max=most).astype(dtype)


def setup_inputs(seed: int = 0) -> dict:
    seeds = jax.random.split(jax.random.key(seed), 6)
    anchor = noise(seeds[0], (REPLICAS, 2, ROWS, D), D ** -0.5, 0.0625, ((0, 64), (2, 8)))
    local_params = draw_local_params(jax.random.fold_in(seeds[5], 71), 0)
    staleness = place_ends(jax.random.randint(seeds[2], (REPLICAS,), 0, 16), jax.random.fold_in(seeds[2], 1), 0, 15).astype(jnp.int32)
    master = noise(seeds[3], (2, ROWS, D), D ** -0.5, 0.0625, ((1, 8), (2, 64)), jnp.float32)
    momentum = noise(seeds[4], (2, ROWS, D), 0.001, 0.006, ((1, 8), (2, 64)), jnp.float32)
    return dict(anchor=anchor, local_params=local_params, staleness=staleness, master=master, momentum=momentum)


def reference(anchor, local_params, staleness, master, momentum):
    weights = 1.0 / jnp.sqrt(1.0 + staleness.astype(jnp.float32))
    total = jnp.sum(weights)

    def accumulate(carry, items):
        weight_one, anchor_one, local_one = items
        delta = anchor_one.astype(jnp.float32) - local_one.astype(jnp.float32)
        rounded = lax.optimization_barrier((weight_one * delta).astype(jnp.bfloat16))
        return (carry + rounded.astype(jnp.float32), None)
    start = jnp.zeros(master.shape, jnp.float32)
    summed, _ = lax.scan(accumulate, start, (weights, anchor, local_params))
    outer_grad = summed / total
    norm_value = jnp.sqrt(jnp.sum(outer_grad * outer_grad))
    limit = 0.001 * jnp.sqrt(jnp.float32(2 * ROWS * D))
    factor = jnp.minimum(jnp.float32(1.0), limit / (norm_value + 1e-06))
    clipped = outer_grad * factor
    new_momentum = 0.9 * momentum + clipped
    new_master = master - 0.7 * (clipped + 0.9 * new_momentum)
    return (new_master.astype(jnp.bfloat16), new_master, new_momentum)
```

```python
import jax
import jax.numpy as jnp
from jax import lax
from jax.sharding import Mesh, PartitionSpec as P

D = 8192
ROWS = 256


def exchange(blocks, axes):
    return lax.all_to_all(blocks, axes, 0, 0, tiled=True)


def copies(block, count):
    return jnp.broadcast_to(block[None], (count,) + block.shape)


def shards(anchor, local_params, staleness, master, momentum):
    weights = 1.0 / jnp.sqrt(1.0 + staleness.astype(jnp.float32))
    total = jnp.sum(weights)
    position = lax.axis_index(("x", "u", "v"))
    mine = lax.axis_index("u")
    own_weight = jnp.sum(jnp.where(jnp.arange(64) == position, weights, 0.0))
    base = master - (0.7 * 0.9 * 0.9) * momentum
    bases = lax.all_gather(base, ("u", "v"), axis=0).reshape(4, 4, 2, 32, 128)
    delta = anchor[0].astype(jnp.float32) - local_params[0].astype(jnp.float32)
    term = (own_weight * delta).astype(jnp.bfloat16)
    term = term.reshape(2, 32, 4, 4, 4, 128).transpose(2, 4, 3, 0, 1, 5).reshape(16, 4, 2, 32, 128)
    near = exchange(term, ("x", "v"))
    partial = jnp.sum(near.astype(jnp.float32), axis=0).astype(jnp.bfloat16)
    far = exchange(copies(partial, 4), "u")
    outer_grad = jnp.sum(far.astype(jnp.float32), axis=0) / total
    squares = jnp.sum(outer_grad * outer_grad)
    parts = exchange(jnp.broadcast_to(squares, (128, 1, 128)), ("x", "v", "y", "c"))
    grads = exchange(copies(outer_grad.astype(jnp.bfloat16), 4), "v")
    norm_value = jnp.sqrt(jnp.sum(parts, axis=0)[0, 0])
    limit = 0.001 * jnp.sqrt(jnp.float32(2 * ROWS * D))
    factor = jnp.minimum(jnp.float32(1.0), limit / (norm_value + 1e-06))
    clipped = lax.dynamic_index_in_dim(outer_grad, mine, 0, keepdims=False) * factor
    new_momentum = 0.9 * momentum + clipped
    new_master = master - 0.7 * (clipped + 0.9 * new_momentum)
    quarter = bases - (0.7 * 1.9 * factor) * grads.transpose(1, 0, 2, 3, 4).astype(jnp.float32)
    quarters = exchange(copies(quarter.astype(jnp.bfloat16), 4), "x")
    new_global = quarters.transpose(3, 4, 0, 1, 2, 5).reshape(2, 32, D)
    return (new_global, new_master, new_momentum)


def solution(mesh):
    split = Mesh(mesh.devices.reshape(4, 4, 4, 4, 2), ("x", "u", "v", "y", "c"))
    replica, fsdp = ("x", "u", "v"), ("y", "c")
    placed = (
        P(replica, None, fsdp, None),
        P(replica, None, fsdp, None),
        P(),
        P(None, fsdp, replica),
        P(None, fsdp, replica),
    )
    return jax.shard_map(
        shards,
        mesh=split,
        in_specs=placed,
        out_specs=(P(None, fsdp, None), P(None, fsdp, replica), P(None, fsdp, replica)),
        check_vma=False,
    )
```

```python
import jax
import jax.numpy as jnp
from jax import lax
from jax.experimental import pallas as pl
from jax.experimental.pallas import tpu as pltpu
from jax.sharding import Mesh, PartitionSpec as P

D = 8192
ROWS = 256
LEVELS = 32000.0
VMEM = pl.BlockSpec(memory_space=pltpu.VMEM)
SMEM = pl.BlockSpec(memory_space=pltpu.SMEM)
PARAMS = pltpu.CompilerParams(vmem_limit_bytes=6 * 2**20)


def exchange(blocks, axes):
    return lax.all_to_all(blocks, axes, 0, 0, tiled=True)


def copies(block, count):
    return jnp.broadcast_to(block[None], (count,) + block.shape)


def weights_of(staleness_ref):
    return 1.0 / jnp.sqrt(1.0 + staleness_ref[...].astype(jnp.float32))


def encode(values):
    largest = jnp.max(jnp.abs(values), axis=0, keepdims=True)
    exponent = jnp.clip(jnp.floor(jnp.log2(largest) + 0.002) + 1.0, -126.0, 128.0)
    half = jnp.exp2(-0.5 * exponent)
    coded = jnp.round(values * half * half * LEVELS)
    return coded.astype(jnp.int32).astype(jnp.int16), exponent


def pack_exponents(exponents):
    rows = jnp.concatenate(exponents + [jnp.zeros((12, 128), jnp.float32)], axis=0)
    return rows.astype(jnp.int32).astype(jnp.int16)


def widen(coded):
    return coded.astype(jnp.int32).astype(jnp.float32)


def decode_sum(ref, block):
    result = None
    for sender in range(4):
        exponent = widen(ref[sender, 256:272, :])[block : block + 1]
        half = jnp.exp2(0.5 * exponent)
        part = widen(ref[sender, 64 * block : 64 * block + 64, :]) * (half * (1.0 / LEVELS)) * half
        result = part if result is None else result + part
    return result


def term_kernel(position_ref, staleness_ref, anchor_ref, local_ref, term_ref):
    weights = weights_of(staleness_ref)
    lane = lax.broadcasted_iota(jnp.int32, (1, 64), 1)
    own = jnp.sum(jnp.where(lane == position_ref[0], weights, 0.0), axis=1, keepdims=True)
    for half in range(2):
        delta = anchor_ref[0, half].astype(jnp.float32) - local_ref[0, half].astype(jnp.float32)
        term_ref[0, half] = (own * delta).astype(jnp.bfloat16)


def near_kernel(near_ref, coded_ref):
    for v in range(4):
        exponents = []
        for u in range(4):
            column = (4 * u + v) * 128
            total = near_ref[0, :, :, column : column + 128].astype(jnp.float32)
            for sender in range(1, 4):
                total = total + near_ref[sender, :, :, column : column + 128].astype(jnp.float32)
            coded_ref[v, 64 * u : 64 * u + 64, :], exponent = encode(total.reshape(64, 128))
            exponents.append(exponent)
        coded_ref[v, 256:272, :] = pack_exponents(exponents)


def far_kernel(coded_ref, master_ref, momentum_ref, out_ref):
    exponents = []
    for u in range(4):
        out_ref[64 * u : 64 * u + 64, :], exponent = encode(decode_sum(coded_ref, u))
        exponents.append(exponent)
    out_ref[256:272, :] = pack_exponents(exponents)
    base = master_ref[...] - (0.7 * 0.9 * 0.9) * momentum_ref[...]
    fixed = jnp.round(base.reshape(64, 128) * 2.0**34).astype(jnp.int32)
    out_ref[272:336, :] = (fixed >> 16).astype(jnp.int16)
    out_ref[336:400, :] = ((fixed & 65535) - 32768).astype(jnp.int16)


def grad_kernel(staleness_ref, far_ref, grad_ref, squares_ref):
    total = jnp.sum(weights_of(staleness_ref), axis=1, keepdims=True)
    squares = jnp.zeros((64, 128), jnp.float32)
    for u in range(4):
        grad = decode_sum(far_ref, u) / total
        grad_ref[u] = grad
        squares = squares + grad * grad
    squares = jnp.sum(jnp.sum(squares, axis=0, keepdims=True), axis=1, keepdims=True)
    squares_ref[...] = jnp.broadcast_to(squares[None], (128, 1, 128))


def update_kernel(mine_ref, parts_ref, grad_ref, far_ref, master_ref, momentum_ref, blocks_ref, new_master_ref, new_momentum_ref):
    norm = jnp.sqrt(jnp.sum(parts_ref[...], axis=0))
    limit = 0.001 * float(2 * ROWS * D) ** 0.5
    factor = jnp.minimum(1.0, limit / (norm + 1e-06))
    for u in range(4):
        high = far_ref[u, 272:336, :].astype(jnp.int32)
        low = far_ref[u, 336:400, :].astype(jnp.int32)
        base = (high * 65536 + (low + 32768)).astype(jnp.float32) * 2.0**-34
        blocks_ref[u] = (base - (0.7 * 1.9) * (grad_ref[u] * factor)).astype(jnp.bfloat16)
    clipped = (grad_ref[mine_ref[0]] * factor).reshape(2, 32, 128)
    new_momentum = 0.9 * momentum_ref[...] + clipped
    new_momentum_ref[...] = new_momentum
    new_master_ref[...] = master_ref[...] - 0.7 * (clipped + 0.9 * new_momentum)


def place_kernel(blocks_ref, out_ref):
    for v in range(4):
        for u in range(4):
            column = (4 * u + v) * 128
            out_ref[:, :, column : column + 128] = blocks_ref[0, v, u].reshape(2, 32, 128)


def shards(anchor, local_params, staleness, master, momentum):
    position = lax.axis_index(("x", "u", "v")).astype(jnp.int32).reshape(1)
    mine = lax.axis_index("u").astype(jnp.int32).reshape(1)
    staleness = staleness.reshape(1, 64)
    f32, bf16, i16 = jnp.float32, jnp.bfloat16, jnp.int16
    term = pl.pallas_call(
        term_kernel,
        grid=(4,),
        out_shape=jax.ShapeDtypeStruct((4, 2, 32, 2048), bf16),
        in_specs=[
            SMEM,
            pl.BlockSpec((1, 64), lambda i: (0, 0)),
            pl.BlockSpec((1, 2, 32, 2048), lambda i: (0, 0, 0, i)),
            pl.BlockSpec((1, 2, 32, 2048), lambda i: (0, 0, 0, i)),
        ],
        out_specs=pl.BlockSpec((1, 2, 32, 2048), lambda i: (i, 0, 0, 0)),
        name="term", compiler_params=PARAMS,
    )(position, staleness, anchor, local_params)
    near = exchange(term, "x")
    coded = pl.pallas_call(
        near_kernel, out_shape=jax.ShapeDtypeStruct((4, 272, 128), i16), in_specs=[VMEM], out_specs=VMEM, name="near", compiler_params=PARAMS,
    )(near)
    coded = exchange(coded, "v")
    packed = pl.pallas_call(
        far_kernel, out_shape=jax.ShapeDtypeStruct((400, 128), i16), in_specs=[VMEM] * 3, out_specs=VMEM, name="far", compiler_params=PARAMS,
    )(coded, master, momentum)
    far = exchange(copies(packed, 4), "u")
    grad, squares = pl.pallas_call(
        grad_kernel,
        out_shape=(jax.ShapeDtypeStruct((4, 64, 128), f32), jax.ShapeDtypeStruct((128, 1, 128), f32)),
        in_specs=[VMEM] * 2,
        out_specs=(VMEM, VMEM),
        name="grad", compiler_params=PARAMS,
    )(staleness, far)
    parts = exchange(squares, ("x", "v", "y", "c"))
    block = jax.ShapeDtypeStruct((2, 32, 128), f32)
    blocks, new_master, new_momentum = pl.pallas_call(
        update_kernel,
        out_shape=(jax.ShapeDtypeStruct((4, 64, 128), bf16), block, block),
        in_specs=[SMEM] + [VMEM] * 5,
        out_specs=(VMEM, VMEM, VMEM),
        name="update", compiler_params=PARAMS,
    )(mine, parts, grad, far, master, momentum)
    quarter = exchange(copies(blocks, 4), "v")
    quarters = exchange(copies(quarter, 4), "x")
    new_global = pl.pallas_call(
        place_kernel,
        grid=(4,),
        out_shape=jax.ShapeDtypeStruct((2, 32, D), bf16),
        in_specs=[pl.BlockSpec((1, 4, 4, 64, 128), lambda i: (i, 0, 0, 0, 0))],
        out_specs=pl.BlockSpec((2, 32, 2048), lambda i: (0, 0, i)),
        name="place", compiler_params=PARAMS,
    )(quarters)
    return (new_global, new_master, new_momentum)


def solution(mesh):
    split = Mesh(mesh.devices.reshape(4, 4, 4, 4, 2), ("x", "u", "v", "y", "c"))
    replica, fsdp = ("x", "u", "v"), ("y", "c")
    placed = (
        P(replica, None, fsdp, None),
        P(replica, None, fsdp, None),
        P(),
        P(None, fsdp, replica),
        P(None, fsdp, replica),
    )
    return jax.shard_map(
        shards,
        mesh=split,
        in_specs=placed,
        out_specs=(P(None, fsdp, None), P(None, fsdp, replica), P(None, fsdp, replica)),
        check_vma=False,
    )
```

```python
import jax
import jax.numpy as jnp
from jax import lax
from jax.experimental import pallas as pl
from jax.experimental.pallas import tpu as pltpu
from jax.sharding import Mesh, PartitionSpec as P

D = 8192
ROWS = 256
LEVELS = 32000.0
VMEM = pl.BlockSpec(memory_space=pltpu.VMEM)
SMEM = pl.BlockSpec(memory_space=pltpu.SMEM)
HBM = pl.BlockSpec(memory_space=pltpu.HBM)


def exchange(blocks, axes):
    return lax.all_to_all(blocks, axes, 0, 0, tiled=True)


def copies(block, count):
    return jnp.broadcast_to(block[None], (count,) + block.shape)


def encode(values):
    largest = jnp.max(jnp.abs(values), axis=0, keepdims=True)
    exponent = jnp.clip(jnp.floor(jnp.log2(largest) + 0.002) + 1.0, -126.0, 128.0)
    half = jnp.exp2(-0.5 * exponent)
    coded = jnp.round(values * half * half * LEVELS)
    return coded.astype(jnp.int32).astype(jnp.int16), exponent


def pack_exponents(exponents):
    rows = exponents + [jnp.zeros((16 - len(exponents), 128), jnp.float32)]
    return jnp.concatenate(rows, axis=0).astype(jnp.int32).astype(jnp.int16)


def widen(coded):
    return coded.astype(jnp.int32).astype(jnp.float32)


def decode(coded, exponent):
    half = jnp.exp2(0.5 * exponent)
    return widen(coded) * (half * (1.0 / LEVELS)) * half


def decode_sum(ref, block):
    result = None
    for sender in range(4):
        exponent = widen(ref[sender, 256:272, :])[block : block + 1]
        part = decode(ref[sender, 64 * block : 64 * block + 64, :], exponent)
        result = part if result is None else result + part
    return result


def term_kernel(position_ref, staleness_ref, anchor_ref, local_ref, term_ref, total_ref, stale, anchors, locals_, sems, stale_sem):
    first = pltpu.make_async_copy(staleness_ref, stale, stale_sem)
    first.start()
    pending = []
    for quarter in range(4):
        columns = pl.ds(2048 * quarter, 2048)
        pair = (
            pltpu.make_async_copy(anchor_ref.at[0, :, :, columns], anchors.at[quarter], sems.at[0, quarter]),
            pltpu.make_async_copy(local_ref.at[0, :, :, columns], locals_.at[quarter], sems.at[1, quarter]),
        )
        pair[0].start()
        pair[1].start()
        pending.append(pair)
    first.wait()
    weights = 1.0 / jnp.sqrt(1.0 + stale[...].astype(jnp.float32))
    lane = lax.broadcasted_iota(jnp.int32, (1, 64), 1)
    own = jnp.sum(jnp.where(lane == position_ref[0], weights, 0.0), axis=1, keepdims=True)
    total_ref[...] = jnp.broadcast_to(jnp.sum(weights, axis=1, keepdims=True), (8, 128))
    for quarter in range(4):
        pending[quarter][0].wait()
        pending[quarter][1].wait()
        for half in range(2):
            delta = anchors[quarter, half].astype(jnp.float32) - locals_[quarter, half].astype(jnp.float32)
            term_ref[quarter, half] = (own * delta).astype(jnp.bfloat16)


def near_kernel(near_ref, coded_ref):
    for v in range(4):
        exponents = []
        for u in range(4):
            column = (4 * u + v) * 128
            total = near_ref[0, :, :, column : column + 128].astype(jnp.float32)
            for sender in range(1, 4):
                total = total + near_ref[sender, :, :, column : column + 128].astype(jnp.float32)
            coded_ref[v, 64 * u : 64 * u + 64, :], exponent = encode(total.reshape(64, 128))
            exponents.append(exponent)
        coded_ref[v, 256:272, :] = pack_exponents(exponents)


def far_kernel(coded_ref, master_ref, momentum_ref, out_ref):
    exponents = []
    for u in range(4):
        out_ref[64 * u : 64 * u + 64, :], exponent = encode(decode_sum(coded_ref, u))
        exponents.append(exponent)
    base = master_ref[...] - (0.7 * 0.9 * 0.9) * momentum_ref[...]
    out_ref[272:336, :], exponent = encode(base.reshape(64, 128))
    out_ref[256:272, :] = pack_exponents(exponents + [exponent])


def grad_kernel(total_ref, far_ref, grad_ref, coded_ref):
    exponents, base_exponents = [], []
    for u in range(4):
        grad = decode_sum(far_ref, u) / total_ref[0:1, :]
        grad_ref[u] = grad
        coded_ref[64 * u : 64 * u + 64, :], exponent = encode(grad)
        exponents.append(exponent)
        coded_ref[272 + 64 * u : 336 + 64 * u, :] = far_ref[u, 272:336, :]
        base_exponents.append(widen(far_ref[u, 256:272, :])[4:5])
    coded_ref[256:272, :] = pack_exponents(exponents + base_exponents)


def grad_of(coded_ref, v, u):
    return decode(coded_ref[v, 64 * u : 64 * u + 64, :], widen(coded_ref[v, 256:272, :])[u : u + 1])


def base_of(coded_ref, v, u):
    return decode(coded_ref[v, 272 + 64 * u : 336 + 64 * u, :], widen(coded_ref[v, 256:272, :])[4 + u : 5 + u])


def squares_kernel(coded_ref, squares_ref):
    squares = jnp.zeros((64, 128), jnp.float32)
    for v in range(4):
        for u in range(4):
            grad = grad_of(coded_ref, v, u)
            squares = squares + grad * grad
    squares = jnp.sum(jnp.sum(squares, axis=0, keepdims=True), axis=1, keepdims=True)
    squares_ref[...] = jnp.broadcast_to(squares[None], (32, 1, 128))


def update_kernel(mine_ref, parts_ref, coded_ref, grad_ref, master_ref, momentum_ref, quarter_ref, new_master_ref, new_momentum_ref):
    norm = jnp.sqrt(jnp.sum(parts_ref[...], axis=0))
    limit = 0.001 * float(2 * ROWS * D) ** 0.5
    factor = jnp.minimum(1.0, limit / (norm + 1e-06))
    for v in range(4):
        for u in range(4):
            column = (4 * u + v) * 128
            value = base_of(coded_ref, v, u) - (0.7 * 1.9) * (grad_of(coded_ref, v, u) * factor)
            quarter_ref[:, :, column : column + 128] = value.astype(jnp.bfloat16).reshape(2, 32, 128)
    clipped = (grad_ref[mine_ref[0]] * factor).reshape(2, 32, 128)
    new_momentum = 0.9 * momentum_ref[...] + clipped
    new_momentum_ref[...] = new_momentum
    new_master_ref[...] = master_ref[...] - 0.7 * (clipped + 0.9 * new_momentum)


def place_kernel(quarters_ref, out_ref, sems):
    pending = []
    for quarter in range(4):
        copy = pltpu.make_async_copy(quarters_ref.at[quarter], out_ref.at[:, :, pl.ds(2048 * quarter, 2048)], sems.at[quarter])
        copy.start()
        pending.append(copy)
    for copy in pending:
        copy.wait()


def call(kernel, name, outs, in_specs, out_specs, scratch=(), mib=6):
    return pl.pallas_call(
        kernel,
        out_shape=[jax.ShapeDtypeStruct(shape, dtype) for shape, dtype in outs],
        in_specs=in_specs,
        out_specs=out_specs,
        scratch_shapes=scratch,
        name=name,
        compiler_params=pltpu.CompilerParams(vmem_limit_bytes=mib * 2**20),
    )


def shards(anchor, local_params, staleness, master, momentum):
    position = lax.axis_index(("x", "u", "v")).astype(jnp.int32).reshape(1)
    mine = lax.axis_index("u").astype(jnp.int32).reshape(1)
    f32, bf16, i16 = jnp.float32, jnp.bfloat16, jnp.int16
    held = pltpu.VMEM((4, 2, 32, 2048), bf16)
    dma = pltpu.SemaphoreType.DMA
    term, total = call(
        term_kernel,
        "term",
        [((4, 2, 32, 2048), bf16), ((8, 128), f32)],
        [SMEM, HBM, HBM, HBM],
        [VMEM, VMEM],
        [pltpu.VMEM((1, 64), jnp.int32), held, held, dma((2, 4)), dma(())],
        mib=56,
    )(position, staleness.reshape(1, 64), anchor, local_params)
    near = exchange(term, "x")
    (coded,) = call(near_kernel, "near", [((4, 272, 128), i16)], [VMEM], [VMEM])(near)
    coded = exchange(coded, "v")
    (packed,) = call(far_kernel, "far", [((336, 128), i16)], [VMEM] * 3, [VMEM])(coded, master, momentum)
    far = lax.all_gather(packed, "u", axis=0)
    grad, coded = call(
        grad_kernel, "grad", [((4, 64, 128), f32), ((528, 128), i16)], [VMEM] * 2, [VMEM] * 2
    )(total, far)
    coded = lax.all_gather(coded, "v", axis=0)
    (squares,) = call(squares_kernel, "squares", [((32, 1, 128), f32)], [VMEM], [VMEM])(coded)
    parts = exchange(squares, ("x", "y", "c"))
    quarter, new_master, new_momentum = call(
        update_kernel,
        "update",
        [((2, 32, 2048), bf16), ((2, 32, 128), f32), ((2, 32, 128), f32)],
        [SMEM] + [VMEM] * 5,
        [VMEM] * 3,
    )(mine, parts, coded, grad, master, momentum)
    quarters = exchange(copies(quarter, 4), "x")
    (new_global,) = call(place_kernel, "place", [((2, 32, D), bf16)], [VMEM], [HBM], [dma((4,))])(quarters)
    return (new_global, new_master, new_momentum)


def solution(mesh):
    split = Mesh(mesh.devices.reshape(4, 4, 4, 4, 2), ("x", "u", "v", "y", "c"))
    replica, fsdp = ("x", "u", "v"), ("y", "c")
    placed = (
        P(replica, None, fsdp, None),
        P(replica, None, fsdp, None),
        P(),
        P(None, fsdp, replica),
        P(None, fsdp, replica),
    )
    return jax.shard_map(
        shards,
        mesh=split,
        in_specs=placed,
        out_specs=(P(None, fsdp, None), P(None, fsdp, replica), P(None, fsdp, replica)),
        check_vma=False,
    )
```

```python
import jax
import jax.numpy as jnp
from jax import lax
from jax.experimental import pallas as pl
from jax.experimental.pallas import tpu as pltpu
from jax.sharding import Mesh, PartitionSpec as P

D = 8192
ROWS = 256
LEVELS = 32000.0
VMEM = pl.BlockSpec(memory_space=pltpu.VMEM)
SMEM = pl.BlockSpec(memory_space=pltpu.SMEM)
HBM = pl.BlockSpec(memory_space=pltpu.HBM)


def exchange(blocks, axes):
    return lax.all_to_all(blocks, axes, 0, 0, tiled=True)


def copies(block, count):
    return jnp.broadcast_to(block[None], (count,) + block.shape)


def encode(values):
    largest = jnp.max(jnp.abs(values), axis=0, keepdims=True)
    exponent = jnp.clip(jnp.floor(jnp.log2(largest) + 0.002) + 1.0, -126.0, 128.0)
    half = jnp.exp2(-0.5 * exponent)
    coded = jnp.round(values * half * half * LEVELS)
    return coded.astype(jnp.int32).astype(jnp.int16), exponent


def pack_exponents(exponents):
    rows = exponents + [jnp.zeros((16 - len(exponents), 128), jnp.float32)]
    return jnp.concatenate(rows, axis=0).astype(jnp.int32).astype(jnp.int16)


def widen(coded):
    return coded.astype(jnp.int32).astype(jnp.float32)


def decode(coded, exponent):
    half = jnp.exp2(0.5 * exponent)
    return widen(coded) * (half * (1.0 / LEVELS)) * half


def decode_sum(ref, senders, block):
    result = None
    for sender in range(senders):
        exponent = widen(ref[sender, 256:272, :])[block : block + 1]
        part = decode(ref[sender, 64 * block : 64 * block + 64, :], exponent)
        result = part if result is None else result + part
    return result


def term_kernel(position_ref, staleness_ref, anchor_ref, local_ref, term_ref, total_ref, stale, anchors, locals_, sems, stale_sem):
    first = pltpu.make_async_copy(staleness_ref, stale, stale_sem)
    first.start()
    pending = []
    for quarter in range(4):
        columns = pl.ds(2048 * quarter, 2048)
        pair = (
            pltpu.make_async_copy(anchor_ref.at[0, :, :, columns], anchors.at[quarter], sems.at[0, quarter]),
            pltpu.make_async_copy(local_ref.at[0, :, :, columns], locals_.at[quarter], sems.at[1, quarter]),
        )
        pair[0].start()
        pair[1].start()
        pending.append(pair)
    first.wait()
    weights = 1.0 / jnp.sqrt(1.0 + stale[...].astype(jnp.float32))
    lane = lax.broadcasted_iota(jnp.int32, (1, 64), 1)
    own = jnp.sum(jnp.where(lane == position_ref[0], weights, 0.0), axis=1, keepdims=True)
    total_ref[...] = jnp.broadcast_to(jnp.sum(weights, axis=1, keepdims=True), (8, 128))
    for quarter in range(4):
        pending[quarter][0].wait()
        pending[quarter][1].wait()
        for half in range(2):
            delta = anchors[quarter, half].astype(jnp.float32) - locals_[quarter, half].astype(jnp.float32)
            term = (own * delta).astype(jnp.bfloat16)
            for z in range(16):
                term_ref[2 * quarter + z % 2, z // 2, half] = term[:, 128 * z : 128 * z + 128]


def near_kernel(near_ref, coded_ref):
    for m in range(2):
        exponents = []
        for u in range(4):
            total = near_ref[0, 2 * u + m].astype(jnp.float32)
            for sender in range(1, 8):
                total = total + near_ref[sender, 2 * u + m].astype(jnp.float32)
            coded_ref[m, 64 * u : 64 * u + 64, :], exponent = encode(total.reshape(64, 128))
            exponents.append(exponent)
        coded_ref[m, 256:272, :] = pack_exponents(exponents)


def far_kernel(coded_ref, master_ref, momentum_ref, out_ref):
    exponents = []
    for u in range(4):
        out_ref[64 * u : 64 * u + 64, :], exponent = encode(decode_sum(coded_ref, 2, u))
        exponents.append(exponent)
    base = master_ref[...] - (0.7 * 0.9 * 0.9) * momentum_ref[...]
    out_ref[272:336, :], exponent = encode(base.reshape(64, 128))
    out_ref[256:272, :] = pack_exponents(exponents + [exponent])


def grad_kernel(total_ref, far_ref, grad_ref, squares_ref):
    squares = jnp.zeros((64, 128), jnp.float32)
    for u in range(4):
        grad = decode_sum(far_ref, 4, u) / total_ref[0:1, :]
        grad_ref[u] = grad
        squares = squares + grad * grad
    squares = jnp.sum(jnp.sum(squares, axis=0, keepdims=True), axis=1, keepdims=True)
    squares_ref[...] = jnp.broadcast_to(squares[None], (128, 1, 128))


def update_kernel(mine_ref, parts_ref, far_ref, grad_ref, master_ref, momentum_ref, blocks_ref, new_master_ref, new_momentum_ref):
    norm = jnp.sqrt(jnp.sum(parts_ref[...], axis=0))
    limit = 0.001 * float(2 * ROWS * D) ** 0.5
    factor = jnp.minimum(1.0, limit / (norm + 1e-06))
    for u in range(4):
        base = decode(far_ref[u, 272:336, :], widen(far_ref[u, 256:272, :])[4:5])
        blocks_ref[u] = (base - (0.7 * 1.9) * (grad_ref[u] * factor)).astype(jnp.bfloat16)
    clipped = (grad_ref[mine_ref[0]] * factor).reshape(2, 32, 128)
    new_momentum = 0.9 * momentum_ref[...] + clipped
    new_momentum_ref[...] = new_momentum
    new_master_ref[...] = master_ref[...] - 0.7 * (clipped + 0.9 * new_momentum)


def place_kernel(blocks_ref, out_ref, quarters, sems):
    pending = []
    for x in range(4):
        for z in range(16):
            block = blocks_ref[2 * x + z % 2, (z // 2) % 2, z // 4]
            quarters[x, :, :, 128 * z : 128 * z + 128] = block.reshape(2, 32, 128)
        copy = pltpu.make_async_copy(quarters.at[x], out_ref.at[:, :, pl.ds(2048 * x, 2048)], sems.at[x])
        copy.start()
        pending.append(copy)
    for copy in pending:
        copy.wait()


def call(kernel, name, outs, in_specs, out_specs, scratch=(), mib=6):
    return pl.pallas_call(
        kernel,
        out_shape=[jax.ShapeDtypeStruct(shape, dtype) for shape, dtype in outs],
        in_specs=in_specs,
        out_specs=out_specs,
        scratch_shapes=scratch,
        name=name,
        compiler_params=pltpu.CompilerParams(vmem_limit_bytes=mib * 2**20),
    )


def shards(anchor, local_params, staleness, master, momentum):
    position = lax.axis_index(("x", "u", "m", "p")).astype(jnp.int32).reshape(1)
    mine = lax.axis_index("u").astype(jnp.int32).reshape(1)
    f32, bf16, i16 = jnp.float32, jnp.bfloat16, jnp.int16
    held = pltpu.VMEM((4, 2, 32, 2048), bf16)
    dma = pltpu.SemaphoreType.DMA
    term, total = call(
        term_kernel,
        "term",
        [((8, 8, 2, 32, 128), bf16), ((8, 128), f32)],
        [SMEM, HBM, HBM, HBM],
        [VMEM, VMEM],
        [pltpu.VMEM((1, 64), jnp.int32), held, held, dma((2, 4)), dma(())],
        mib=56,
    )(position, staleness.reshape(1, 64), anchor, local_params)
    near = exchange(term, ("x", "p"))
    (coded,) = call(near_kernel, "near", [((2, 272, 128), i16)], [VMEM], [VMEM])(near)
    coded = exchange(coded, "m")
    (packed,) = call(far_kernel, "far", [((336, 128), i16)], [VMEM] * 3, [VMEM])(coded, master, momentum)
    far = lax.all_gather(packed, "u", axis=0)
    grad, squares = call(
        grad_kernel, "grad", [((4, 64, 128), f32), ((128, 1, 128), f32)], [VMEM] * 2, [VMEM] * 2
    )(total, far)
    parts = exchange(squares, ("x", "m", "p", "y", "c"))
    blocks, new_master, new_momentum = call(
        update_kernel,
        "update",
        [((4, 64, 128), bf16), ((2, 32, 128), f32), ((2, 32, 128), f32)],
        [SMEM] + [VMEM] * 5,
        [VMEM] * 3,
    )(mine, parts, far, grad, master, momentum)
    blocks = lax.all_gather(blocks, "m", axis=0)
    blocks = exchange(copies(blocks, 8), ("x", "p"))
    (new_global,) = call(place_kernel, "place", [((2, 32, D), bf16)], [VMEM], [HBM], [held, dma((4,))])(blocks.reshape(8, 2, 4, 64, 128))
    return (new_global, new_master, new_momentum)


def solution(mesh):
    split = Mesh(mesh.devices.reshape(4, 4, 2, 2, 4, 2), ("x", "u", "m", "p", "y", "c"))
    replica, fsdp = ("x", "u", "m", "p"), ("y", "c")
    placed = (
        P(replica, None, fsdp, None),
        P(replica, None, fsdp, None),
        P(),
        P(None, fsdp, replica),
        P(None, fsdp, replica),
    )
    return jax.shard_map(
        shards,
        mesh=split,
        in_specs=placed,
        out_specs=(P(None, fsdp, None), P(None, fsdp, replica), P(None, fsdp, replica)),
        check_vma=False,
    )
```

```python
import jax
import jax.numpy as jnp
from jax import lax
from jax.experimental import pallas as pl
from jax.experimental.pallas import tpu as pltpu
from jax.sharding import Mesh, PartitionSpec as P

D = 8192
ROWS = 256
LEVELS = 32000.0
VMEM = pl.BlockSpec(memory_space=pltpu.VMEM)
SMEM = pl.BlockSpec(memory_space=pltpu.SMEM)
HBM = pl.BlockSpec(memory_space=pltpu.HBM)


def exchange(blocks, axes):
    return lax.all_to_all(blocks, axes, 0, 0, tiled=True)


def copies(block, count):
    return jnp.broadcast_to(block[None], (count,) + block.shape)


def encode(values):
    largest = jnp.max(jnp.abs(values), axis=0, keepdims=True)
    exponent = jnp.clip(jnp.floor(jnp.log2(largest) + 0.002) + 1.0, -126.0, 128.0)
    half = jnp.exp2(-0.5 * exponent)
    coded = jnp.round(values * half * half * LEVELS)
    return coded.astype(jnp.int32).astype(jnp.int16), exponent


def pack_exponents(exponents):
    rows = exponents + [jnp.zeros((16 - len(exponents), 128), jnp.float32)]
    return jnp.concatenate(rows, axis=0).astype(jnp.int32).astype(jnp.int16)


def widen(coded):
    return coded.astype(jnp.int32).astype(jnp.float32)


def decode(coded, exponent):
    half = jnp.exp2(0.5 * exponent)
    return widen(coded) * (half * (1.0 / LEVELS)) * half


def decode_sum(ref, senders, block):
    result = None
    for sender in range(senders):
        exponent = widen(ref[sender, 256:272, :])[block : block + 1]
        part = decode(ref[sender, 64 * block : 64 * block + 64, :], exponent)
        result = part if result is None else result + part
    return result


def term_kernel(position_ref, staleness_ref, anchor_ref, local_ref, term_ref, total_ref, stale, anchors, locals_, sems, stale_sem):
    first = pltpu.make_async_copy(staleness_ref, stale, stale_sem)
    first.start()
    pending = []
    for quarter in range(4):
        columns = pl.ds(2048 * quarter, 2048)
        pair = (
            pltpu.make_async_copy(anchor_ref.at[0, :, :, columns], anchors.at[quarter], sems.at[0, quarter]),
            pltpu.make_async_copy(local_ref.at[0, :, :, columns], locals_.at[quarter], sems.at[1, quarter]),
        )
        pair[0].start()
        pair[1].start()
        pending.append(pair)
    first.wait()
    weights = 1.0 / jnp.sqrt(1.0 + stale[...].astype(jnp.float32))
    lane = lax.broadcasted_iota(jnp.int32, (1, 64), 1)
    own = jnp.sum(jnp.where(lane == position_ref[0], weights, 0.0), axis=1, keepdims=True)
    total_ref[...] = jnp.broadcast_to(jnp.sum(weights, axis=1, keepdims=True), (8, 128))
    for quarter in range(4):
        pending[quarter][0].wait()
        pending[quarter][1].wait()
        for half in range(2):
            delta = anchors[quarter, half].astype(jnp.float32) - locals_[quarter, half].astype(jnp.float32)
            term = (own * delta).astype(jnp.bfloat16)
            for z in range(16):
                term_ref[2 * quarter + z % 2, z // 2, half] = term[:, 128 * z : 128 * z + 128]


def near_kernel(near_ref, coded_ref):
    for m in range(2):
        exponents = []
        for u in range(4):
            total = near_ref[0, 2 * u + m].astype(jnp.float32)
            for sender in range(1, 8):
                total = total + near_ref[sender, 2 * u + m].astype(jnp.float32)
            coded_ref[m, 64 * u : 64 * u + 64, :], exponent = encode(total.reshape(64, 128))
            exponents.append(exponent)
        coded_ref[m, 256:272, :] = pack_exponents(exponents)


def far_kernel(coded_ref, master_ref, momentum_ref, out_ref):
    exponents = []
    for u in range(4):
        out_ref[64 * u : 64 * u + 64, :], exponent = encode(decode_sum(coded_ref, 2, u))
        exponents.append(exponent)
    base = master_ref[...] - (0.7 * 0.9 * 0.9) * momentum_ref[...]
    out_ref[272:336, :], exponent = encode(base.reshape(64, 128))
    out_ref[256:272, :] = pack_exponents(exponents + [exponent])


def grad_kernel(total_ref, far_ref, grad_ref, coded_ref, squares_ref):
    squares = jnp.zeros((64, 128), jnp.float32)
    exponents, base_exponents = [], []
    for u in range(4):
        grad = decode_sum(far_ref, 4, u) / total_ref[0:1, :]
        grad_ref[u] = grad
        squares = squares + grad * grad
        coded_ref[64 * u : 64 * u + 64, :], exponent = encode(grad)
        exponents.append(exponent)
        coded_ref[272 + 64 * u : 336 + 64 * u, :] = far_ref[u, 272:336, :]
        base_exponents.append(widen(far_ref[u, 256:272, :])[4:5])
    coded_ref[256:272, :] = pack_exponents(exponents + base_exponents)
    squares = jnp.sum(jnp.sum(squares, axis=0, keepdims=True), axis=1, keepdims=True)
    squares_ref[...] = jnp.broadcast_to(squares[None], (128, 1, 128))


def update_kernel(mine_ref, parts_ref, coded_ref, grad_ref, master_ref, momentum_ref, blocks_ref, new_master_ref, new_momentum_ref):
    norm = jnp.sqrt(jnp.sum(parts_ref[...], axis=0))
    limit = 0.001 * float(2 * ROWS * D) ** 0.5
    factor = jnp.minimum(1.0, limit / (norm + 1e-06))
    for m in range(2):
        exponents = widen(coded_ref[m, 256:272, :])
        for u in range(4):
            base = decode(coded_ref[m, 272 + 64 * u : 336 + 64 * u, :], exponents[4 + u : 5 + u])
            grad = decode(coded_ref[m, 64 * u : 64 * u + 64, :], exponents[u : u + 1])
            blocks_ref[m, u] = (base - (0.7 * 1.9) * (grad * factor)).astype(jnp.bfloat16)
    clipped = (grad_ref[mine_ref[0]] * factor).reshape(2, 32, 128)
    new_momentum = 0.9 * momentum_ref[...] + clipped
    new_momentum_ref[...] = new_momentum
    new_master_ref[...] = master_ref[...] - 0.7 * (clipped + 0.9 * new_momentum)


def place_kernel(blocks_ref, out_ref, quarters, sems):
    pending = []
    for x in range(4):
        for z in range(16):
            block = blocks_ref[2 * x + z % 2, (z // 2) % 2, z // 4]
            quarters[x, :, :, 128 * z : 128 * z + 128] = block.reshape(2, 32, 128)
        copy = pltpu.make_async_copy(quarters.at[x], out_ref.at[:, :, pl.ds(2048 * x, 2048)], sems.at[x])
        copy.start()
        pending.append(copy)
    for copy in pending:
        copy.wait()


def call(kernel, name, outs, in_specs, out_specs, scratch=(), mib=6):
    return pl.pallas_call(
        kernel,
        out_shape=[jax.ShapeDtypeStruct(shape, dtype) for shape, dtype in outs],
        in_specs=in_specs,
        out_specs=out_specs,
        scratch_shapes=scratch,
        name=name,
        compiler_params=pltpu.CompilerParams(vmem_limit_bytes=mib * 2**20),
    )


def shards(anchor, local_params, staleness, master, momentum):
    position = lax.axis_index(("x", "u", "m", "p")).astype(jnp.int32).reshape(1)
    mine = lax.axis_index("u").astype(jnp.int32).reshape(1)
    f32, bf16, i16 = jnp.float32, jnp.bfloat16, jnp.int16
    held = pltpu.VMEM((4, 2, 32, 2048), bf16)
    dma = pltpu.SemaphoreType.DMA
    term, total = call(
        term_kernel,
        "term",
        [((8, 8, 2, 32, 128), bf16), ((8, 128), f32)],
        [SMEM, HBM, HBM, HBM],
        [VMEM, VMEM],
        [pltpu.VMEM((1, 64), jnp.int32), held, held, dma((2, 4)), dma(())],
        mib=56,
    )(position, staleness.reshape(1, 64), anchor, local_params)
    near = exchange(term, ("x", "p"))
    (coded,) = call(near_kernel, "near", [((2, 272, 128), i16)], [VMEM], [VMEM])(near)
    coded = exchange(coded, "m")
    (packed,) = call(far_kernel, "far", [((336, 128), i16)], [VMEM] * 3, [VMEM])(coded, master, momentum)
    far = lax.all_gather(packed, "u", axis=0)
    grad, coded, squares = call(
        grad_kernel,
        "grad",
        [((4, 64, 128), f32), ((528, 128), i16), ((128, 1, 128), f32)],
        [VMEM] * 2,
        [VMEM] * 3,
    )(total, far)
    parts = exchange(squares, ("x", "m", "p", "y", "c"))
    coded = lax.all_gather(coded, "m", axis=0)
    blocks, new_master, new_momentum = call(
        update_kernel,
        "update",
        [((2, 4, 64, 128), bf16), ((2, 32, 128), f32), ((2, 32, 128), f32)],
        [SMEM] + [VMEM] * 5,
        [VMEM] * 3,
    )(mine, parts, coded, grad, master, momentum)
    blocks = exchange(copies(blocks, 8), ("x", "p"))
    (new_global,) = call(place_kernel, "place", [((2, 32, D), bf16)], [VMEM], [HBM], [held, dma((4,))])(blocks.reshape(8, 2, 4, 64, 128))
    return (new_global, new_master, new_momentum)


def solution(mesh):
    split = Mesh(mesh.devices.reshape(4, 4, 2, 2, 4, 2), ("x", "u", "m", "p", "y", "c"))
    replica, fsdp = ("x", "u", "m", "p"), ("y", "c")
    placed = (
        P(replica, None, fsdp, None),
        P(replica, None, fsdp, None),
        P(),
        P(None, fsdp, replica),
        P(None, fsdp, replica),
    )
    return jax.shard_map(
        shards,
        mesh=split,
        in_specs=placed,
        out_specs=(P(None, fsdp, None), P(None, fsdp, replica), P(None, fsdp, replica)),
        check_vma=False,
    )
```

```python
import jax
import jax.numpy as jnp
from jax import lax
from jax.experimental import pallas as pl
from jax.experimental.pallas import tpu as pltpu
from jax.sharding import Mesh, PartitionSpec as P

D = 8192
ROWS = 256
LEVELS = 32000.0
VMEM = pl.BlockSpec(memory_space=pltpu.VMEM)
SMEM = pl.BlockSpec(memory_space=pltpu.SMEM)
HBM = pl.BlockSpec(memory_space=pltpu.HBM)


def exchange(blocks, axes):
    return lax.all_to_all(blocks, axes, 0, 0, tiled=True)


def copies(block, count):
    return jnp.broadcast_to(block[None], (count,) + block.shape)


def encode(values):
    largest = jnp.max(jnp.abs(values), axis=0, keepdims=True)
    exponent = jnp.clip(jnp.floor(jnp.log2(largest) + 0.002) + 1.0, -126.0, 128.0)
    half = jnp.exp2(-0.5 * exponent)
    coded = jnp.round(values * half * half * LEVELS)
    return coded.astype(jnp.int32).astype(jnp.int16), exponent


def pack_exponents(exponents):
    rows = exponents + [jnp.zeros((16 - len(exponents), 128), jnp.float32)]
    return jnp.concatenate(rows, axis=0).astype(jnp.int32).astype(jnp.int16)


def widen(coded):
    return coded.astype(jnp.int32).astype(jnp.float32)


def decode(coded, exponent):
    half = jnp.exp2(0.5 * exponent)
    return widen(coded) * (half * (1.0 / LEVELS)) * half


def decode_sum(ref, senders, block):
    result = None
    for sender in range(senders):
        exponent = widen(ref[sender, 256:272, :])[block : block + 1]
        part = decode(ref[sender, 64 * block : 64 * block + 64, :], exponent)
        result = part if result is None else result + part
    return result


def term_kernel(position_ref, staleness_ref, anchor_ref, local_ref, term_ref, total_ref, stale, anchors, locals_, sems, stale_sem):
    first = pltpu.make_async_copy(staleness_ref, stale, stale_sem)
    first.start()
    pending = []
    for quarter in range(4):
        columns = pl.ds(2048 * quarter, 2048)
        pair = (
            pltpu.make_async_copy(anchor_ref.at[0, :, :, columns], anchors.at[quarter], sems.at[0, quarter]),
            pltpu.make_async_copy(local_ref.at[0, :, :, columns], locals_.at[quarter], sems.at[1, quarter]),
        )
        pair[0].start()
        pair[1].start()
        pending.append(pair)
    first.wait()
    weights = 1.0 / jnp.sqrt(1.0 + stale[...].astype(jnp.float32))
    lane = lax.broadcasted_iota(jnp.int32, (1, 64), 1)
    own = jnp.sum(jnp.where(lane == position_ref[0], weights, 0.0), axis=1, keepdims=True)
    total_ref[...] = jnp.broadcast_to(jnp.sum(weights, axis=1, keepdims=True), (8, 128))
    for quarter in range(4):
        pending[quarter][0].wait()
        pending[quarter][1].wait()
        for half in range(2):
            delta = anchors[quarter, half].astype(jnp.float32) - locals_[quarter, half].astype(jnp.float32)
            term = (own * delta).astype(jnp.bfloat16)
            for z in range(16):
                term_ref[2 * quarter + z % 2, z // 2, half] = term[:, 128 * z : 128 * z + 128]


def near_kernel(near_ref, bases_ref, coded_ref, packed_ref):
    for m in range(2):
        exponents = []
        for u in range(4):
            total = near_ref[0, 2 * u + m].astype(jnp.float32)
            for sender in range(1, 8):
                total = total + near_ref[sender, 2 * u + m].astype(jnp.float32)
            coded_ref[m, 64 * u : 64 * u + 64, :], exponent = encode(total.reshape(64, 128))
            exponents.append(exponent)
        coded_ref[m, 256:272, :] = pack_exponents(exponents)
    exponents = []
    for m in range(2):
        packed_ref[64 * m : 64 * m + 64, :] = bases_ref[m, :64, :]
        exponents.append(widen(bases_ref[m, 64:80, :])[0:1])
    packed_ref[128:144, :] = pack_exponents(exponents)


def base_kernel(master_ref, momentum_ref, out_ref):
    base = master_ref[...] - (0.7 * 0.9 * 0.9) * momentum_ref[...]
    out_ref[:64, :], exponent = encode(base.reshape(64, 128))
    out_ref[64:80, :] = pack_exponents([exponent])


def far_kernel(coded_ref, bases_ref, out_ref):
    exponents = []
    for u in range(4):
        out_ref[64 * u : 64 * u + 64, :], exponent = encode(decode_sum(coded_ref, 2, u))
        exponents.append(exponent)
    out_ref[272:400, :] = bases_ref[:128, :]
    base_exponents = widen(bases_ref[128:144, :])
    out_ref[256:272, :] = pack_exponents(exponents + [base_exponents[0:1], base_exponents[1:2]])


def grad_kernel(total_ref, far_ref, grad_ref, coded_ref, squares_ref):
    squares = jnp.zeros((64, 128), jnp.float32)
    exponents = []
    for u in range(4):
        grad = decode_sum(far_ref, 4, u) / total_ref[0:1, :]
        grad_ref[u] = grad
        squares = squares + grad * grad
        coded_ref[64 * u : 64 * u + 64, :], exponent = encode(grad)
        exponents.append(exponent)
    coded_ref[256:272, :] = pack_exponents(exponents)
    squares = jnp.sum(jnp.sum(squares, axis=0, keepdims=True), axis=1, keepdims=True)
    squares_ref[...] = jnp.broadcast_to(squares[None], (128, 1, 128))


def update_kernel(mine_ref, parts_ref, far_ref, coded_ref, grad_ref, master_ref, momentum_ref, blocks_ref, new_master_ref, new_momentum_ref):
    norm = jnp.sqrt(jnp.sum(parts_ref[...], axis=0))
    limit = 0.001 * float(2 * ROWS * D) ** 0.5
    factor = jnp.minimum(1.0, limit / (norm + 1e-06))
    for m in range(2):
        exponents = widen(coded_ref[m, 256:272, :])
        for u in range(4):
            base_exponents = widen(far_ref[u, 256:272, :])
            base = decode(far_ref[u, 272 + 64 * m : 336 + 64 * m, :], base_exponents[4 + m : 5 + m])
            grad = decode(coded_ref[m, 64 * u : 64 * u + 64, :], exponents[u : u + 1])
            blocks_ref[m, u] = (base - (0.7 * 1.9) * (grad * factor)).astype(jnp.bfloat16)
    clipped = (grad_ref[mine_ref[0]] * factor).reshape(2, 32, 128)
    new_momentum = 0.9 * momentum_ref[...] + clipped
    new_momentum_ref[...] = new_momentum
    new_master_ref[...] = master_ref[...] - 0.7 * (clipped + 0.9 * new_momentum)


def place_kernel(blocks_ref, out_ref, quarters, sems):
    pending = []
    for x in range(4):
        for z in range(16):
            block = blocks_ref[2 * x + z % 2, (z // 2) % 2, z // 4]
            quarters[x, :, :, 128 * z : 128 * z + 128] = block.reshape(2, 32, 128)
        copy = pltpu.make_async_copy(quarters.at[x], out_ref.at[:, :, pl.ds(2048 * x, 2048)], sems.at[x])
        copy.start()
        pending.append(copy)
    for copy in pending:
        copy.wait()


def call(kernel, name, outs, in_specs, out_specs, scratch=(), mib=6):
    return pl.pallas_call(
        kernel,
        out_shape=[jax.ShapeDtypeStruct(shape, dtype) for shape, dtype in outs],
        in_specs=in_specs,
        out_specs=out_specs,
        scratch_shapes=scratch,
        name=name,
        compiler_params=pltpu.CompilerParams(vmem_limit_bytes=mib * 2**20),
    )


def shards(anchor, local_params, staleness, master, momentum):
    position = lax.axis_index(("x", "u", "m", "p")).astype(jnp.int32).reshape(1)
    mine = lax.axis_index("u").astype(jnp.int32).reshape(1)
    f32, bf16, i16 = jnp.float32, jnp.bfloat16, jnp.int16
    held = pltpu.VMEM((4, 2, 32, 2048), bf16)
    dma = pltpu.SemaphoreType.DMA
    term, total = call(
        term_kernel,
        "term",
        [((8, 8, 2, 32, 128), bf16), ((8, 128), f32)],
        [SMEM, HBM, HBM, HBM],
        [VMEM, VMEM],
        [pltpu.VMEM((1, 64), jnp.int32), held, held, dma((2, 4)), dma(())],
        mib=56,
    )(position, staleness.reshape(1, 64), anchor, local_params)
    near = exchange(term, ("x", "p"))
    (base,) = call(base_kernel, "base", [((80, 128), i16)], [VMEM] * 2, [VMEM])(master, momentum)
    bases = lax.all_gather(base, "m", axis=0)
    coded, bases = call(
        near_kernel, "near", [((2, 272, 128), i16), ((144, 128), i16)], [VMEM] * 2, [VMEM] * 2
    )(near, bases)
    coded = exchange(coded, "m")
    (packed,) = call(far_kernel, "far", [((400, 128), i16)], [VMEM] * 2, [VMEM])(coded, bases)
    far = lax.all_gather(packed, "u", axis=0)
    grad, coded, squares = call(
        grad_kernel,
        "grad",
        [((4, 64, 128), f32), ((272, 128), i16), ((128, 1, 128), f32)],
        [VMEM] * 2,
        [VMEM] * 3,
    )(total, far)
    parts = exchange(squares, ("x", "m", "p", "y", "c"))
    coded = lax.all_gather(coded, "m", axis=0)
    blocks, new_master, new_momentum = call(
        update_kernel,
        "update",
        [((2, 4, 64, 128), bf16), ((2, 32, 128), f32), ((2, 32, 128), f32)],
        [SMEM] + [VMEM] * 6,
        [VMEM] * 3,
    )(mine, parts, far, coded, grad, master, momentum)
    blocks = exchange(copies(blocks, 8), ("x", "p"))
    (new_global,) = call(place_kernel, "place", [((2, 32, D), bf16)], [VMEM], [HBM], [held, dma((4,))])(blocks.reshape(8, 2, 4, 64, 128))
    return (new_global, new_master, new_momentum)


def solution(mesh):
    split = Mesh(mesh.devices.reshape(4, 4, 2, 2, 4, 2), ("x", "u", "m", "p", "y", "c"))
    replica, fsdp = ("x", "u", "m", "p"), ("y", "c")
    placed = (
        P(replica, None, fsdp, None),
        P(replica, None, fsdp, None),
        P(),
        P(None, fsdp, replica),
        P(None, fsdp, replica),
    )
    return jax.shard_map(
        shards,
        mesh=split,
        in_specs=placed,
        out_specs=(P(None, fsdp, None), P(None, fsdp, replica), P(None, fsdp, replica)),
        check_vma=False,
    )
```

```python
import jax
import jax.numpy as jnp
from jax import lax
from jax.experimental import pallas as pl
from jax.experimental.pallas import tpu as pltpu
from jax.sharding import Mesh, PartitionSpec as P

D = 8192
ROWS = 256
LEVELS = 32000.0
VMEM = pl.BlockSpec(memory_space=pltpu.VMEM)
SMEM = pl.BlockSpec(memory_space=pltpu.SMEM)
HBM = pl.BlockSpec(memory_space=pltpu.HBM)


def exchange(blocks, axes):
    return lax.all_to_all(blocks, axes, 0, 0, tiled=True)


def copies(block, count):
    return jnp.broadcast_to(block[None], (count,) + block.shape)


def encode(values):
    largest = jnp.max(jnp.abs(values), axis=0, keepdims=True)
    exponent = jnp.clip(jnp.floor(jnp.log2(largest) + 0.002) + 1.0, -126.0, 128.0)
    half = jnp.exp2(-0.5 * exponent)
    coded = jnp.round(values * half * half * LEVELS)
    return coded.astype(jnp.int32).astype(jnp.int16), exponent


def pack_exponents(exponents):
    rows = exponents + [jnp.zeros((16 - len(exponents), 128), jnp.float32)]
    return jnp.concatenate(rows, axis=0).astype(jnp.int32).astype(jnp.int16)


def widen(coded):
    return coded.astype(jnp.int32).astype(jnp.float32)


def decode(coded, exponent):
    half = jnp.exp2(0.5 * exponent)
    return widen(coded) * (half * (1.0 / LEVELS)) * half


def decode_sum(ref, senders, block):
    result = None
    for sender in range(senders):
        exponent = widen(ref[sender, 256:272, :])[block : block + 1]
        part = decode(ref[sender, 64 * block : 64 * block + 64, :], exponent)
        result = part if result is None else result + part
    return result


def term_kernel(position_ref, staleness_ref, anchor_ref, local_ref, term_ref, total_ref, stale, anchors, locals_, sems, stale_sem):
    first = pltpu.make_async_copy(staleness_ref, stale, stale_sem)
    first.start()
    pending = []
    for quarter in range(4):
        columns = pl.ds(2048 * quarter, 2048)
        pair = (
            pltpu.make_async_copy(anchor_ref.at[0, :, :, columns], anchors.at[quarter], sems.at[0, quarter]),
            pltpu.make_async_copy(local_ref.at[0, :, :, columns], locals_.at[quarter], sems.at[1, quarter]),
        )
        pair[0].start()
        pair[1].start()
        pending.append(pair)
    first.wait()
    weights = 1.0 / jnp.sqrt(1.0 + stale[...].astype(jnp.float32))
    lane = lax.broadcasted_iota(jnp.int32, (1, 64), 1)
    own = jnp.sum(jnp.where(lane == position_ref[0], weights, 0.0), axis=1, keepdims=True)
    total_ref[...] = jnp.broadcast_to(jnp.sum(weights, axis=1, keepdims=True), (8, 128))
    for quarter in range(4):
        pending[quarter][0].wait()
        pending[quarter][1].wait()
        for half in range(2):
            delta = anchors[quarter, half].astype(jnp.float32) - locals_[quarter, half].astype(jnp.float32)
            term = (own * delta).astype(jnp.bfloat16)
            for z in range(16):
                term_ref[2 * quarter + z % 2, z // 2, half] = term[:, 128 * z : 128 * z + 128]


def near_kernel(near_ref, bases_ref, coded_ref, packed_ref):
    for m in range(2):
        exponents = []
        for u in range(4):
            total = near_ref[0, 2 * u + m].astype(jnp.float32)
            for sender in range(1, 8):
                total = total + near_ref[sender, 2 * u + m].astype(jnp.float32)
            coded_ref[m, 64 * u : 64 * u + 64, :], exponent = encode(total.reshape(64, 128))
            exponents.append(exponent)
        coded_ref[m, 256:272, :] = pack_exponents(exponents)
    exponents = []
    for m in range(2):
        packed_ref[64 * m : 64 * m + 64, :] = bases_ref[m, :64, :]
        exponents.append(widen(bases_ref[m, 64:80, :])[0:1])
    packed_ref[128:144, :] = pack_exponents(exponents)


def base_kernel(master_ref, momentum_ref, out_ref):
    base = master_ref[...] - (0.7 * 0.9 * 0.9) * momentum_ref[...]
    out_ref[:64, :], exponent = encode(base.reshape(64, 128))
    out_ref[64:80, :] = pack_exponents([exponent])


def far_kernel(coded_ref, bases_ref, out_ref):
    exponents = []
    for u in range(4):
        out_ref[64 * u : 64 * u + 64, :], exponent = encode(decode_sum(coded_ref, 2, u))
        exponents.append(exponent)
    out_ref[272:400, :] = bases_ref[:128, :]
    base_exponents = widen(bases_ref[128:144, :])
    out_ref[256:272, :] = pack_exponents(exponents + [base_exponents[0:1], base_exponents[1:2]])


def grad_kernel(total_ref, far_ref, grad_ref, coded_ref, squares_ref, held, sem):
    squares = jnp.zeros((64, 128), jnp.float32)
    for u in range(4):
        grad = decode_sum(far_ref, 4, u) / total_ref[0:1, :]
        grad_ref[u] = grad
        squares = squares + grad * grad
    squares = jnp.sum(jnp.sum(squares, axis=0, keepdims=True), axis=1, keepdims=True)
    held[...] = jnp.broadcast_to(squares[None], (128, 1, 128))
    copy = pltpu.make_async_copy(held, squares_ref, sem)
    copy.start()
    exponents = []
    for u in range(4):
        coded_ref[64 * u : 64 * u + 64, :], exponent = encode(grad_ref[u])
        exponents.append(exponent)
    coded_ref[256:272, :] = pack_exponents(exponents)
    copy.wait()


def update_kernel(mine_ref, parts_ref, far_ref, coded_ref, grad_ref, master_ref, momentum_ref, blocks_ref, new_master_ref, new_momentum_ref, held, sems):
    norm = jnp.sqrt(jnp.sum(parts_ref[...], axis=0))
    limit = 0.001 * float(2 * ROWS * D) ** 0.5
    factor = jnp.minimum(1.0, limit / (norm + 1e-06))
    clipped = (grad_ref[mine_ref[0]] * factor).reshape(2, 32, 128)
    new_momentum = 0.9 * momentum_ref[...] + clipped
    held[0] = new_momentum
    held[1] = master_ref[...] - 0.7 * (clipped + 0.9 * new_momentum)
    pending = [
        pltpu.make_async_copy(held.at[0], new_momentum_ref, sems.at[0]),
        pltpu.make_async_copy(held.at[1], new_master_ref, sems.at[1]),
    ]
    for copy in pending:
        copy.start()
    for m in range(2):
        exponents = widen(coded_ref[m, 256:272, :])
        for u in range(4):
            base_exponents = widen(far_ref[u, 256:272, :])
            base = decode(far_ref[u, 272 + 64 * m : 336 + 64 * m, :], base_exponents[4 + m : 5 + m])
            grad = decode(coded_ref[m, 64 * u : 64 * u + 64, :], exponents[u : u + 1])
            blocks_ref[m, u] = (base - (0.7 * 1.9) * (grad * factor)).astype(jnp.bfloat16)
    for copy in pending:
        copy.wait()


def place_kernel(blocks_ref, out_ref, quarters, sems):
    pending = []
    for x in range(4):
        for z in range(16):
            block = blocks_ref[2 * x + z % 2, (z // 2) % 2, z // 4]
            quarters[x, :, :, 128 * z : 128 * z + 128] = block.reshape(2, 32, 128)
        copy = pltpu.make_async_copy(quarters.at[x], out_ref.at[:, :, pl.ds(2048 * x, 2048)], sems.at[x])
        copy.start()
        pending.append(copy)
    for copy in pending:
        copy.wait()


def call(kernel, name, outs, in_specs, out_specs, scratch=(), mib=6):
    return pl.pallas_call(
        kernel,
        out_shape=[jax.ShapeDtypeStruct(shape, dtype) for shape, dtype in outs],
        in_specs=in_specs,
        out_specs=out_specs,
        scratch_shapes=scratch,
        name=name,
        compiler_params=pltpu.CompilerParams(vmem_limit_bytes=mib * 2**20),
    )


def shards(anchor, local_params, staleness, master, momentum):
    position = lax.axis_index(("x", "u", "m", "p")).astype(jnp.int32).reshape(1)
    mine = lax.axis_index("u").astype(jnp.int32).reshape(1)
    f32, bf16, i16 = jnp.float32, jnp.bfloat16, jnp.int16
    held = pltpu.VMEM((4, 2, 32, 2048), bf16)
    dma = pltpu.SemaphoreType.DMA
    term, total = call(
        term_kernel,
        "term",
        [((8, 8, 2, 32, 128), bf16), ((8, 128), f32)],
        [SMEM, HBM, HBM, HBM],
        [VMEM, VMEM],
        [pltpu.VMEM((1, 64), jnp.int32), held, held, dma((2, 4)), dma(())],
        mib=56,
    )(position, staleness.reshape(1, 64), anchor, local_params)
    near = exchange(term, ("x", "p"))
    (base,) = call(base_kernel, "base", [((80, 128), i16)], [VMEM] * 2, [VMEM])(master, momentum)
    bases = lax.all_gather(base, "m", axis=0)
    coded, bases = call(
        near_kernel, "near", [((2, 272, 128), i16), ((144, 128), i16)], [VMEM] * 2, [VMEM] * 2
    )(near, bases)
    coded = exchange(coded, "m")
    (packed,) = call(far_kernel, "far", [((400, 128), i16)], [VMEM] * 2, [VMEM])(coded, bases)
    far = lax.all_gather(packed, "u", axis=0)
    grad, coded, squares = call(
        grad_kernel,
        "grad",
        [((4, 64, 128), f32), ((272, 128), i16), ((128, 1, 128), f32)],
        [VMEM] * 2,
        [VMEM, VMEM, HBM],
        [pltpu.VMEM((128, 1, 128), f32), dma(())],
    )(total, far)
    parts = exchange(squares, ("x", "m", "p", "y", "c"))
    coded = lax.all_gather(coded, "m", axis=0)
    blocks, new_master, new_momentum = call(
        update_kernel,
        "update",
        [((2, 4, 64, 128), bf16), ((2, 32, 128), f32), ((2, 32, 128), f32)],
        [SMEM] + [VMEM] * 6,
        [VMEM, HBM, HBM],
        [pltpu.VMEM((2, 2, 32, 128), f32), dma((2,))],
    )(mine, parts, far, coded, grad, master, momentum)
    blocks = exchange(copies(blocks, 8), ("x", "p"))
    (new_global,) = call(place_kernel, "place", [((2, 32, D), bf16)], [VMEM], [HBM], [held, dma((4,))])(blocks.reshape(8, 2, 4, 64, 128))
    return (new_global, new_master, new_momentum)


def solution(mesh):
    split = Mesh(mesh.devices.reshape(4, 4, 2, 2, 4, 2), ("x", "u", "m", "p", "y", "c"))
    replica, fsdp = ("x", "u", "m", "p"), ("y", "c")
    placed = (
        P(replica, None, fsdp, None),
        P(replica, None, fsdp, None),
        P(),
        P(None, fsdp, replica),
        P(None, fsdp, replica),
    )
    return jax.shard_map(
        shards,
        mesh=split,
        in_specs=placed,
        out_specs=(P(None, fsdp, None), P(None, fsdp, replica), P(None, fsdp, replica)),
        check_vma=False,
    )
```

```python
import jax
import jax.numpy as jnp
from jax import lax
from jax.experimental import pallas as pl
from jax.experimental.pallas import tpu as pltpu
from jax.sharding import Mesh, PartitionSpec as P

D = 8192
ROWS = 256
LEVELS = 32000.0
VMEM = pl.BlockSpec(memory_space=pltpu.VMEM)
SMEM = pl.BlockSpec(memory_space=pltpu.SMEM)
HBM = pl.BlockSpec(memory_space=pltpu.HBM)


def exchange(blocks, axes):
    return lax.all_to_all(blocks, axes, 0, 0, tiled=True)


def copies(block, count):
    return jnp.broadcast_to(block[None], (count,) + block.shape)


def encode(values):
    largest = jnp.max(jnp.abs(values), axis=0, keepdims=True)
    exponent = jnp.clip(jnp.floor(jnp.log2(largest) + 0.002) + 1.0, -126.0, 128.0)
    half = jnp.exp2(-0.5 * exponent)
    coded = jnp.round(values * half * half * LEVELS)
    return coded.astype(jnp.int32).astype(jnp.int16), exponent


def pack_exponents(exponents):
    rows = exponents + [jnp.zeros((16 - len(exponents), 128), jnp.float32)]
    return jnp.concatenate(rows, axis=0).astype(jnp.int32).astype(jnp.int16)


def widen(coded):
    return coded.astype(jnp.int32).astype(jnp.float32)


def decode(coded, exponent):
    half = jnp.exp2(0.5 * exponent)
    return widen(coded) * (half * (1.0 / LEVELS)) * half


def decode_sum(ref, senders, block):
    result = None
    for sender in range(senders):
        exponent = widen(ref[sender, 256:272, :])[block : block + 1]
        part = decode(ref[sender, 64 * block : 64 * block + 64, :], exponent)
        result = part if result is None else result + part
    return result


def term_kernel(position_ref, staleness_ref, anchor_ref, local_ref, term_ref, total_ref, stale, anchors, locals_, sems, stale_sem):
    first = pltpu.make_async_copy(staleness_ref, stale, stale_sem)
    first.start()
    pending = []
    for quarter in range(4):
        columns = pl.ds(2048 * quarter, 2048)
        pair = (
            pltpu.make_async_copy(anchor_ref.at[0, :, :, columns], anchors.at[quarter], sems.at[0, quarter]),
            pltpu.make_async_copy(local_ref.at[0, :, :, columns], locals_.at[quarter], sems.at[1, quarter]),
        )
        pair[0].start()
        pair[1].start()
        pending.append(pair)
    first.wait()
    weights = 1.0 / jnp.sqrt(1.0 + stale[...].astype(jnp.float32))
    lane = lax.broadcasted_iota(jnp.int32, (1, 64), 1)
    own = jnp.sum(jnp.where(lane == position_ref[0], weights, 0.0), axis=1, keepdims=True)
    total_ref[...] = jnp.broadcast_to(jnp.sum(weights, axis=1, keepdims=True), (8, 128))
    for quarter in range(4):
        pending[quarter][0].wait()
        pending[quarter][1].wait()
        for half in range(2):
            delta = anchors[quarter, half].astype(jnp.float32) - locals_[quarter, half].astype(jnp.float32)
            term = (own * delta).astype(jnp.bfloat16)
            for z in range(16):
                term_ref[2 * quarter + z % 2, z // 2, half] = term[:, 128 * z : 128 * z + 128]


def near_kernel(near_ref, bases_ref, coded_ref, packed_ref):
    for m in range(2):
        exponents = []
        for u in range(4):
            total = near_ref[0, 2 * u + m].astype(jnp.float32)
            for sender in range(1, 8):
                total = total + near_ref[sender, 2 * u + m].astype(jnp.float32)
            coded_ref[m, 64 * u : 64 * u + 64, :], exponent = encode(total.reshape(64, 128))
            exponents.append(exponent)
        coded_ref[m, 256:272, :] = pack_exponents(exponents)
    exponents = []
    for m in range(2):
        packed_ref[64 * m : 64 * m + 64, :] = bases_ref[m, :64, :]
        exponents.append(widen(bases_ref[m, 64:80, :])[0:1])
    packed_ref[128:144, :] = pack_exponents(exponents)


def base_kernel(master_ref, momentum_ref, out_ref):
    base = master_ref[...] - (0.7 * 0.9 * 0.9) * momentum_ref[...]
    out_ref[:64, :], exponent = encode(base.reshape(64, 128))
    out_ref[64:80, :] = pack_exponents([exponent])


def far_kernel(coded_ref, bases_ref, out_ref):
    exponents = []
    for u in range(4):
        out_ref[64 * u : 64 * u + 64, :], exponent = encode(decode_sum(coded_ref, 2, u))
        exponents.append(exponent)
    out_ref[272:400, :] = bases_ref[:128, :]
    base_exponents = widen(bases_ref[128:144, :])
    out_ref[256:272, :] = pack_exponents(exponents + [base_exponents[0:1], base_exponents[1:2]])


def grad_kernel(total_ref, far_ref, grad_ref, coded_ref, squares_ref):
    squares = jnp.zeros((64, 128), jnp.float32)
    exponents = []
    for u in range(4):
        grad = decode_sum(far_ref, 4, u) / total_ref[0:1, :]
        grad_ref[u] = grad
        squares = squares + grad * grad
        coded_ref[64 * u : 64 * u + 64, :], exponent = encode(grad)
        exponents.append(exponent)
    coded_ref[256:272, :] = pack_exponents(exponents)
    squares = jnp.sum(jnp.sum(squares, axis=0, keepdims=True), axis=1, keepdims=True)
    squares_ref[...] = jnp.broadcast_to(squares[None], (128, 1, 128))


def factor_of(parts_ref):
    norm = jnp.sqrt(jnp.sum(parts_ref[...], axis=0))
    limit = 0.001 * float(2 * ROWS * D) ** 0.5
    return jnp.minimum(1.0, limit / (norm + 1e-06))


def update_kernel(parts_ref, far_ref, coded_ref, blocks_ref):
    factor = factor_of(parts_ref)
    for m in range(2):
        exponents = widen(coded_ref[m, 256:272, :])
        for u in range(4):
            base_exponents = widen(far_ref[u, 256:272, :])
            base = decode(far_ref[u, 272 + 64 * m : 336 + 64 * m, :], base_exponents[4 + m : 5 + m])
            grad = decode(coded_ref[m, 64 * u : 64 * u + 64, :], exponents[u : u + 1])
            blocks_ref[m, u] = (base - (0.7 * 1.9) * (grad * factor)).astype(jnp.bfloat16)


def place_kernel(mine_ref, blocks_ref, parts_ref, grad_ref, master_ref, momentum_ref, out_ref, new_master_ref, new_momentum_ref, quarters, held, sems, own_sems):
    pending = []
    for x in range(4):
        for z in range(16):
            block = blocks_ref[2 * x + z % 2, (z // 2) % 2, z // 4]
            quarters[x, :, :, 128 * z : 128 * z + 128] = block.reshape(2, 32, 128)
        copy = pltpu.make_async_copy(quarters.at[x], out_ref.at[:, :, pl.ds(2048 * x, 2048)], sems.at[x])
        copy.start()
        pending.append(copy)
    clipped = (grad_ref[mine_ref[0]] * factor_of(parts_ref)).reshape(2, 32, 128)
    new_momentum = 0.9 * momentum_ref[...] + clipped
    held[0] = new_momentum
    held[1] = master_ref[...] - 0.7 * (clipped + 0.9 * new_momentum)
    for row, ref in enumerate((new_momentum_ref, new_master_ref)):
        copy = pltpu.make_async_copy(held.at[row], ref, own_sems.at[row])
        copy.start()
        pending.append(copy)
    for copy in pending:
        copy.wait()


def call(kernel, name, outs, in_specs, out_specs, scratch=(), mib=6):
    return pl.pallas_call(
        kernel,
        out_shape=[jax.ShapeDtypeStruct(shape, dtype) for shape, dtype in outs],
        in_specs=in_specs,
        out_specs=out_specs,
        scratch_shapes=scratch,
        name=name,
        compiler_params=pltpu.CompilerParams(vmem_limit_bytes=mib * 2**20),
    )


def shards(anchor, local_params, staleness, master, momentum):
    position = lax.axis_index(("x", "u", "m", "p")).astype(jnp.int32).reshape(1)
    mine = lax.axis_index("u").astype(jnp.int32).reshape(1)
    f32, bf16, i16 = jnp.float32, jnp.bfloat16, jnp.int16
    held = pltpu.VMEM((4, 2, 32, 2048), bf16)
    dma = pltpu.SemaphoreType.DMA
    term, total = call(
        term_kernel,
        "term",
        [((8, 8, 2, 32, 128), bf16), ((8, 128), f32)],
        [SMEM, HBM, HBM, HBM],
        [VMEM, VMEM],
        [pltpu.VMEM((1, 64), jnp.int32), held, held, dma((2, 4)), dma(())],
        mib=56,
    )(position, staleness.reshape(1, 64), anchor, local_params)
    near = exchange(term, ("x", "p"))
    (base,) = call(base_kernel, "base", [((80, 128), i16)], [VMEM] * 2, [VMEM])(master, momentum)
    bases = lax.all_gather(base, "m", axis=0)
    coded, bases = call(
        near_kernel, "near", [((2, 272, 128), i16), ((144, 128), i16)], [VMEM] * 2, [VMEM] * 2
    )(near, bases)
    coded = exchange(coded, "m")
    (packed,) = call(far_kernel, "far", [((400, 128), i16)], [VMEM] * 2, [VMEM])(coded, bases)
    far = lax.all_gather(packed, "u", axis=0)
    grad, coded, squares = call(
        grad_kernel,
        "grad",
        [((4, 64, 128), f32), ((272, 128), i16), ((128, 1, 128), f32)],
        [VMEM] * 2,
        [VMEM] * 3,
    )(total, far)
    parts = exchange(squares, ("x", "m", "p", "y", "c"))
    coded = lax.all_gather(coded, "m", axis=0)
    (blocks,) = call(update_kernel, "update", [((2, 4, 64, 128), bf16)], [VMEM] * 3, [VMEM])(parts, far, coded)
    blocks = exchange(copies(blocks, 8), ("x", "p")).reshape(8, 2, 4, 64, 128)
    block = ((2, 32, 128), f32)
    new_global, new_master, new_momentum = call(
        place_kernel,
        "place",
        [((2, 32, D), bf16), block, block],
        [SMEM] + [VMEM] * 5,
        [HBM] * 3,
        [held, pltpu.VMEM((2, 2, 32, 128), f32), dma((4,)), dma((2,))],
    )(mine, blocks, parts, grad, master, momentum)
    return (new_global, new_master, new_momentum)


def solution(mesh):
    split = Mesh(mesh.devices.reshape(4, 4, 2, 2, 4, 2), ("x", "u", "m", "p", "y", "c"))
    replica, fsdp = ("x", "u", "m", "p"), ("y", "c")
    placed = (
        P(replica, None, fsdp, None),
        P(replica, None, fsdp, None),
        P(),
        P(None, fsdp, replica),
        P(None, fsdp, replica),
    )
    return jax.shard_map(
        shards,
        mesh=split,
        in_specs=placed,
        out_specs=(P(None, fsdp, None), P(None, fsdp, replica), P(None, fsdp, replica)),
        check_vma=False,
    )
```
